32 devices in a mesh: group: 2 (over x), row: 8 (over z, y), col: 2 (over core).
Axes of the slice: x: 2, y: 2, z: 4, core: 2. Of those that a mesh axis runs over, the one named last changes fastest.
Arguments:
- anomalies: bfloat16 [32, 65536], P('group', ('row', 'col')), parts along dimension 0, may hold values from -6 to 6
- order: int32 [16, 4096], P(('row', 'col')), may hold values from 0 to 4095, each once within a row
- bases: bfloat16 [256, 64, 256], P(('row', 'col')), may hold values from -0.375 to 0.375
- near_blocks: bfloat16 [256, 3, 256, 256], P(('row', 'col')), may hold values from -0.21875 to 0.21875
- far_rows: int32 [16, 256], P(('row', 'col')), may hold values from -1 to 255, as said below
- far_cols: int32 [16, 256], P(('row', 'col')), may hold values from -1 to 255, as said below
- coupling: bfloat16 [16, 256, 4096], P(('row', 'col')), may hold values from -0.75 to 0.75
Outputs:
- covaried: bfloat16 [32, 65536], P('group', ('row', 'col')), parts along dimension 0
The draws below stay inside these ranges and needn't reach their ends.
There are 2 independent parts, one for each index of `group`. The reference program is written for one: setup_inputs(seed, part) draws one part's arguments, and reference() takes and returns one part's arrays. A program takes and returns all parts, laid end to end along the dimension named above; an argument that names none is the same for every part. Nothing has to cross between parts.
Inputs may be any that keep to these rules, and one draw needn't show every extreme that they name: `far_rows`: slots of device block d name leaves d * 16 to (d + 1) * 16 - 1; each block's live slots come first, then -1; one block in every draw fills all 256 slots. `far_cols`: -1 exactly where far_rows is -1; a live column leaf never lies on the device block of its row leaf; the live column leaves of one device block that lie on any one device block are at most 4 distinct leaves, and some pair of blocks reaches 4 in every draw.
All inputs are finite; a program needn't handle non-finite values.
Results may differ from the reference program's by a relative error of at most 0.0054.
Values may be sent and summed in bfloat16 or wider, within the bound.
A program may use at most 64 MiB of HBM per device.

```python
import jax
import jax.numpy as jnp
from jax import lax

LEAF = 256
RANK = 64
MEMBERS = 16
LEAF_DEV = 16
TASK_DEV = 256
NEED = 4
SHARDS = 16
LEAVES = 256
PTS_DEV = 4096
POINTS = 65536


def task_lists(key):
    busiest = jax.random.randint(jax.random.fold_in(key, 1), (), 0, SHARDS)
    counts = TASK_DEV // 3 + jax.random.randint(jax.random.fold_in(key, 2), (SHARDS,), 0, TASK_DEV // 2)
    counts = jnp.where(jnp.arange(SHARDS) == busiest, TASK_DEV, counts)
    local = jax.random.randint(jax.random.fold_in(key, 3), (SHARDS, TASK_DEV), 0, LEAF_DEV)
    devices = jnp.arange(SHARDS)[:, None]
    task_rows = local + devices * LEAF_DEV
    slot = jnp.arange(TASK_DEV)[None, :]
    live = slot < counts[:, None]
    owners = (devices + 1 + jax.random.randint(jax.random.fold_in(key, 4), (SHARDS, TASK_DEV), 0, SHARDS - 1)) % SHARDS
    starts = jax.random.randint(jax.random.fold_in(key, 5), (SHARDS, SHARDS), 0, LEAF_DEV)
    picks = jax.random.randint(jax.random.fold_in(key, 6), (SHARDS, TASK_DEV), 0, NEED)
    before = (slot == NEED) & (devices >= 0)
    owners = jnp.where(before, (devices + SHARDS - 1) % SHARDS, owners)
    forced = (devices == busiest) & (slot < NEED)
    far_owner = (busiest + SHARDS // 2) % SHARDS
    owners = jnp.where(forced, far_owner, owners)
    picks = jnp.where(forced, slot, picks)
    base = jnp.take_along_axis(starts, owners, axis=1)
    task_cols = owners * LEAF_DEV + (base + picks) % LEAF_DEV
    return (live, task_rows, task_cols)


def draw_far_rows(key, part):
    live, task_rows, task_cols = task_lists(key)
    return jnp.where(live, task_rows, -1).astype(jnp.int32)


def draw_far_cols(key, part):
    live, task_rows, task_cols = task_lists(key)
    return jnp.where(live, task_cols, -1).astype(jnp.int32)


def levels(own_key, extent, shards, low, top_value):
    def one(dim, shards_of):
        draws = jax.random.uniform(jax.random.fold_in(jax.random.fold_in(own_key, 6), dim), (shards_of,), jnp.float32, low / len(shards), top_value / len(shards))
        return jnp.repeat(jnp.exp(draws), extent[dim] // shards_of).reshape((-1,) + (1,) * (len(extent) - dim - 1))

    level = one(*shards[0])
    for cut in shards[1:]:
        level = level * one(*cut)
    return level


def normal_values(key, dims, scale, bound, shards=(), kind=jnp.bfloat16):
    gain = levels(key, dims, shards, -0.22, 0.18) if shards else 1.0
    drawn = jax.random.normal(key, dims, jnp.float32) * scale * gain
    return jnp.minimum(jnp.maximum(drawn, -bound), bound).astype(kind)


def setup_inputs(seed: int = 0, part: int = 0) -> dict:
    key_list = jax.random.split(jax.random.key(seed), 8)
    part_keys = jax.random.split(jax.random.fold_in(key_list[7], part), 8)
    anomalies = normal_values(part_keys[0], (MEMBERS, POINTS), 1.0, 6.0, ((1, 16),))
    order = jax.vmap(lambda own: jax.random.permutation(own, PTS_DEV))(jax.random.split(key_list[1], SHARDS)).reshape((SHARDS, PTS_DEV)).astype(jnp.int32)
    bases = normal_values(key_list[2], (LEAVES, RANK, LEAF), LEAF ** -0.5, 0.375, ((0, 16),))
    near_blocks = normal_values(key_list[3], (LEAVES, 3, LEAF, LEAF), (3 * LEAF) ** -0.5, 0.21875, ((0, 16),))
    far_rows = draw_far_rows(jax.random.fold_in(key_list[7], 71), part)
    far_cols = draw_far_cols(jax.random.fold_in(key_list[7], 71), part)
    coupling = normal_values(key_list[6], (SHARDS, TASK_DEV, RANK * RANK), RANK ** -0.5, 0.75, ((0, 16),))
    return {"anomalies": anomalies, "order": order, "bases": bases, "near_blocks": near_blocks, "far_rows": far_rows, "far_cols": far_cols, "coupling": coupling}


def reference(anomalies, order, bases, near_blocks, far_rows, far_cols, coupling):
    members = anomalies.shape[0]
    offsets = jnp.arange(SHARDS, dtype=jnp.int32) * PTS_DEV
    position = (order + offsets[:, None]).reshape(-1).astype(jnp.int32)
    tree_field = anomalies[:, position]
    leaf_field = tree_field.reshape(members, LEAVES, LEAF).astype(jnp.float32)
    base_values = bases.astype(jnp.float32)
    upward = jnp.einsum('tra,kta->tkr', base_values, leaf_field).astype(jnp.bfloat16)
    upward = upward.reshape(LEAVES, members * RANK)
    zero_leaf = jnp.zeros((members, 1, LEAF), jnp.float32)
    padded = jnp.concatenate([zero_leaf, leaf_field, zero_leaf], axis=1)
    near_field = jnp.zeros((members, LEAVES, LEAF), jnp.float32)
    for offset_index in range(3):
        near_field = near_field + jnp.einsum('tab,ktb->kta', near_blocks[:, offset_index].astype(jnp.float32), padded[:, offset_index:offset_index + LEAVES])

    def one_shard(totals, pieces):
        task_rows, task_cols, matrices = pieces
        live = task_rows >= 0
        picked = upward[jnp.where(live, task_cols, 0)].astype(jnp.float32).reshape(TASK_DEV, members, RANK)
        mats = matrices.astype(jnp.float32).reshape(TASK_DEV, RANK, RANK)
        terms = jnp.einsum('tab,tkb->tka', mats, picked).reshape(TASK_DEV, members * RANK)
        targets = jnp.where(live, task_rows, LEAVES).astype(jnp.int32)
        return totals.at[targets].add(terms, mode='drop'), None

    initial = jnp.zeros((LEAVES, members * RANK), jnp.float32)
    totals, unused = lax.scan(one_shard, initial, (far_rows, far_cols, coupling))
    far_coeffs = totals.astype(jnp.bfloat16).reshape(LEAVES, members, RANK)
    far_field = jnp.einsum('tra,tkr->kta', base_values, far_coeffs.astype(jnp.float32))
    combined = (near_field + far_field).reshape(members, POINTS).astype(jnp.bfloat16)
    return jnp.zeros_like(anomalies).at[:, position].set(combined)
```

```python
import functools

import jax
import jax.numpy as jnp
from jax import lax
from jax.experimental import pallas as pl
from jax.experimental.pallas import tpu as pltpu
from jax.sharding import PartitionSpec as P

NEED = 4
LANES = 128
F32 = jnp.float32
BF16 = jnp.bfloat16
LAST = (((1,), (1,)), ((), ()))
FIRST = (((0,), (0,)), ((), ()))


def dot(x, y):
    return jnp.dot(x, y, preferred_element_type=F32)


def dot_last(x, y):
    return lax.dot_general(x, y, LAST, preferred_element_type=F32)


def iota(shape, dim):
    return lax.broadcasted_iota(jnp.int32, shape, dim)


def flag(condition):
    return jnp.where(condition, 1.0, 0.0).astype(BF16)


def kernel(
    n, inner, members, leaves, rank, leaf, tasks,
    anomalies, order, bases_hbm, near_hbm, far_rows, far_cols, coupling_hbm,
    out,
    bases, near, coupling, cols_all, halo, tree, one_hot, selector, chosen, table,
    turned, picked, near_field, placing, combined,
    load_sems, near_sems, cols_send, cols_recv, halo_send, halo_recv, coef_send, coef_recv,
):
    me = lax.axis_index("row") * inner + lax.axis_index("col")
    width = leaves * leaf
    split = leaf // rank
    groups = members // split
    rows = NEED * groups
    per = leaf // rows
    blocks = n // per
    halves = tasks // LANES

    def at(index):
        return {"row": index // inner, "col": lax.rem(index, inner)}

    def peer(step):
        return lax.rem(me + step, n)

    barrier = pltpu.get_barrier_semaphore()

    def greet(step, carry):
        pl.semaphore_signal(barrier, inc=1, device_id=at(peer(step)), device_id_type=pl.DeviceIdType.MESH)
        return carry

    lax.fori_loop(1, n, greet, 0)

    load_bases = pltpu.make_async_copy(bases_hbm, bases, load_sems.at[0])
    load_bases.start()
    quarter = leaves // 4
    loads = []
    for q in range(4):
        part = pl.ds(q * quarter, quarter)
        loads.append(pltpu.make_async_copy(near_hbm.at[part], near.at[part], near_sems.at[q]))
        loads[-1].start()
    load_coupling = pltpu.make_async_copy(coupling_hbm.at[0], coupling, load_sems.at[1])
    load_coupling.start()

    position = order[...]
    low = position % leaf
    high = position // leaf
    for c in range(leaves):
        piece = slice(c * leaf, (c + 1) * leaf)
        one_hot[:, piece] = flag(iota((leaf, leaf), 0) == low[:, piece])

    pl.semaphore_wait(barrier, n - 1)

    def cols_copy(step):
        return pltpu.make_async_remote_copy(
            src_ref=far_cols, dst_ref=cols_all.at[me],
            send_sem=cols_send.at[step], recv_sem=cols_recv.at[step],
            device_id=at(peer(step)), device_id_type=pl.DeviceIdType.MESH,
        )

    def cols_start(step, carry):
        cols_copy(step).start()
        return carry

    lax.fori_loop(1, n, cols_start, 0)
    cols_all[me] = jnp.full((1, tasks), -1, jnp.int32)

    stacked = jnp.concatenate(
        [anomalies[:, s * leaf : (s + 1) * leaf] for s in range(leaves)], axis=0
    )
    for c in range(leaves):
        piece = slice(c * leaf, (c + 1) * leaf)
        spread = dot(stacked, one_hot[:, piece])
        where_high = high[:, piece]
        total = jnp.zeros((members, leaf), F32)
        for s in range(leaves):
            total = total + jnp.where(where_high == s, spread[s * members : (s + 1) * members], 0.0)
        tree[:, piece] = total.astype(BF16)

    to_next = pltpu.make_async_remote_copy(
        src_ref=tree.at[:, pl.ds((leaves - 1) * leaf, leaf)], dst_ref=halo.at[0],
        send_sem=halo_send.at[0], recv_sem=halo_recv.at[0],
        device_id=at(peer(1)), device_id_type=pl.DeviceIdType.MESH,
    )
    to_before = pltpu.make_async_remote_copy(
        src_ref=tree.at[:, pl.ds(0, leaf)], dst_ref=halo.at[1],
        send_sem=halo_send.at[1], recv_sem=halo_recv.at[1],
        device_id=at(peer(n - 1)), device_id_type=pl.DeviceIdType.MESH,
    )
    to_next.start()
    to_before.start()

    load_bases.wait()
    upward = jnp.concatenate(
        [dot_last(tree[:, t * leaf : (t + 1) * leaf], bases[t]) for t in range(leaves)], axis=0
    ).astype(BF16)
    repeat = flag(iota((rank, leaf), 0) == iota((rank, leaf), 1) % rank)
    square = (leaf, leaf)
    row, col = iota(square, 0), iota(square, 1)
    spread = dot(upward, repeat)
    placed = jnp.where(row % split == col // rank, spread, 0.0).astype(BF16)

    same = row // rows == col // rows
    gather = flag(same)
    earlier = flag(same & (col < row))
    ones = jnp.ones((tasks, leaf), BF16)
    slot = (row % rows) // groups + 1
    group_row = row % groups

    def ranks(hits):
        needed = jnp.minimum(dot(hits, ones), 1.0)
        return needed, dot(earlier, needed.astype(BF16)) + 1.0

    def cols_wait(step, carry):
        cols_copy(step).wait()
        return carry

    lax.fori_loop(1, n, cols_wait, 0)
    slot_f = slot.astype(F32)
    diagonal = row % leaves == col // members
    same_group = group_row == (col % members) // split
    for c in range(blocks):
        wanted = jnp.concatenate(
            [jnp.broadcast_to(cols_all[c * per + d], (leaves, tasks)) for d in range(per)], axis=0
        )
        hits = flag(wanted == iota((leaf, tasks), 0) % leaves + me * leaves)
        needed, numbered = ranks(hits)
        values = jnp.where(diagonal, needed * numbered, 0.0).astype(BF16)
        rank_of = dot(gather, values)
        selection = flag((rank_of == slot_f) & same_group)
        chosen[c * leaf : (c + 1) * leaf, :] = dot(selection, placed).astype(BF16)

    def coef_copy(step):
        there = peer(step)
        return pltpu.make_async_remote_copy(
            src_ref=chosen.at[pl.ds(pl.multiple_of(there * rows, rows), rows)],
            dst_ref=table.at[pl.ds(pl.multiple_of(me * rows, rows), rows)],
            send_sem=coef_send.at[step], recv_sem=coef_recv.at[step],
            device_id=at(there), device_id_type=pl.DeviceIdType.MESH,
        )

    def coef_start(step, carry):
        coef_copy(step).start()
        return carry

    lax.fori_loop(1, n, coef_start, 0)
    table[pl.ds(pl.multiple_of(me * rows, rows), rows), :] = jnp.zeros((rows, leaf), BF16)

    own = far_cols[...]
    for c in range(blocks):
        hits = own == iota((leaf, tasks), 0) + c * leaf
        needed, numbered = ranks(flag(hits))
        rank_of = dot(gather, jnp.where(hits, numbered, 0.0).astype(BF16))
        selector[c * leaf : (c + 1) * leaf, :] = jnp.where(rank_of == slot_f, 1.0, 0.0).astype(BF16)
    placing[...] = flag(far_rows[...] == iota((leaf, tasks), 0) // members + me * leaves)

    to_next.wait()
    to_before.wait()
    before = jnp.where(me > 0, halo[0].astype(F32), 0.0).astype(BF16)
    after = jnp.where(me < n - 1, halo[1].astype(F32), 0.0).astype(BF16)
    for t in range(leaves):
        if t % quarter == 0:
            loads[t // quarter].wait()
        total = jnp.zeros((members, leaf), F32)
        for j in range(3):
            s = t + j - 1
            if s < 0:
                x = before
            elif s >= leaves:
                x = after
            else:
                x = tree[:, s * leaf : (s + 1) * leaf]
            total = total + dot_last(x, near[t, j])
        near_field[:, t * leaf : (t + 1) * leaf] = total

    load_coupling.wait()
    identity = flag(row == col)
    for c in range(rank * rank // leaf):
        piece = slice(c * leaf, (c + 1) * leaf)
        flipped = dot_last(identity, coupling[:, piece])
        for h in range(halves):
            turned[h, piece, :] = flipped[:, h * LANES : (h + 1) * LANES]

    def coef_wait(step, carry):
        coef_copy(step).wait()
        return carry

    lax.fori_loop(1, n, coef_wait, 0)
    for g in range(groups):
        total = jnp.zeros((leaf, tasks), F32)
        for c in range(blocks):
            chunk = slice(c * leaf, (c + 1) * leaf)
            taken = jnp.where(group_row == g, selector[chunk, :].astype(F32), 0.0).astype(BF16)
            total = total + lax.dot_general(table[chunk, :], taken, FIRST, preferred_element_type=F32)
        for h in range(halves):
            picked[h, g * leaf : (g + 1) * leaf, :] = total[:, h * LANES : (h + 1) * LANES]

    together = 4

    def advance(step, total):
        left = []
        right = []
        for u in range(together):
            b = step * together + u
            for h in range(halves):
                values = picked[h, pl.ds(b, members, stride=rank), :].astype(BF16)
                mask = placing[:, h * LANES : (h + 1) * LANES]
                left.append(jnp.concatenate([values] * leaves, axis=0) * mask)
                right.append(turned[h, pl.ds(b, rank, stride=rank), :].astype(BF16))
        return total + dot_last(jnp.concatenate(left, axis=1), jnp.concatenate(right, axis=1))

    far = lax.fori_loop(0, rank // together, advance, jnp.zeros((leaves * members, rank), F32))
    far = far.astype(BF16)
    for t in range(leaves):
        piece = slice(t * leaf, (t + 1) * leaf)
        value = near_field[:, piece] + dot(far[t * members : (t + 1) * members], bases[t])
        combined[:, piece] = value.astype(BF16)

    total = jnp.zeros((leaves * members, leaf), F32)
    for c in range(leaves):
        piece = slice(c * leaf, (c + 1) * leaf)
        values = combined[:, piece].astype(F32)
        where_high = high[:, piece]
        left = jnp.concatenate(
            [jnp.where(where_high == s, values, 0.0).astype(BF16) for s in range(leaves)], axis=0
        )
        total = total + dot_last(left, one_hot[:, piece])
    for s in range(leaves):
        out[:, s * leaf : (s + 1) * leaf] = total[s * members : (s + 1) * members].astype(BF16)


def body(n, inner, anomalies, order, bases, near_blocks, far_rows, far_cols, coupling):
    members, points = anomalies.shape
    leaves, rank, leaf = bases.shape
    tasks = far_cols.shape[1]
    rows = NEED * members * rank // leaf
    vmem = pl.BlockSpec(memory_space=pltpu.VMEM)
    hbm = pl.BlockSpec(memory_space=pl.ANY)
    dma = pltpu.SemaphoreType.DMA
    return pl.pallas_call(
        functools.partial(kernel, n, inner, members, leaves, rank, leaf, tasks),
        out_shape=jax.ShapeDtypeStruct((members, points), BF16),
        in_specs=[vmem, vmem, hbm, hbm, vmem, vmem, hbm],
        out_specs=vmem,
        scratch_shapes=[
            pltpu.VMEM(bases.shape, BF16),
            pltpu.VMEM(near_blocks.shape, BF16),
            pltpu.VMEM((tasks, rank * rank), BF16),
            pltpu.VMEM((n, 1, tasks), jnp.int32),
            pltpu.VMEM((2, members, leaf), BF16),
            pltpu.VMEM((members, points), BF16),
            pltpu.VMEM((leaf, points), BF16),
            pltpu.VMEM((n * rows, tasks), BF16),
            pltpu.VMEM((n * rows, leaf), BF16),
            pltpu.VMEM((n * rows, leaf), BF16),
            pltpu.VMEM((tasks // LANES, rank * rank, LANES), F32),
            pltpu.VMEM((tasks // LANES, members * rank, LANES), F32),
            pltpu.VMEM((members, points), F32),
            pltpu.VMEM((leaves * members, tasks), BF16),
            pltpu.VMEM((members, points), BF16),
            dma((2,)), dma((4,)), dma((n,)), dma((n,)), dma((2,)), dma((2,)), dma((n,)), dma((n,)),
        ],
        compiler_params=pltpu.CompilerParams(
            collective_id=0, has_side_effects=True, vmem_limit_bytes=40 * 1024 * 1024
        ),
    )(anomalies, order, bases, near_blocks, far_rows, far_cols, coupling)


def solution(mesh):
    rows, inner = mesh.shape["row"], mesh.shape["col"]
    spread = ("row", "col")
    in_specs = (
        P("group", spread),
        P(spread, None),
        P(spread, None, None),
        P(spread, None, None, None),
        P(spread, None),
        P(spread, None),
        P(spread, None, None),
    )
    return jax.shard_map(
        functools.partial(body, rows * inner, inner),
        mesh=mesh, in_specs=in_specs, out_specs=P("group", spread), check_vma=False,
    )
```

```python
import functools

import jax
import jax.numpy as jnp
from jax import lax
from jax.experimental import pallas as pl
from jax.experimental.pallas import tpu as pltpu
from jax.sharding import PartitionSpec as P

NEED = 4
LANES = 128
F32 = jnp.float32
BF16 = jnp.bfloat16
LAST = (((1,), (1,)), ((), ()))
FIRST = (((0,), (0,)), ((), ()))


def dot(x, y):
    return jnp.dot(x, y, preferred_element_type=F32)


def dot_last(x, y):
    return lax.dot_general(x, y, LAST, preferred_element_type=F32)


def iota(shape, dim):
    return lax.broadcasted_iota(jnp.int32, shape, dim)


def flag(condition):
    return jnp.where(condition, 1.0, 0.0).astype(BF16)


def kernel(
    n, inner, members, leaves, rank, leaf, tasks,
    anomalies_hbm, order_hbm, bases_hbm, near_hbm, far_rows_hbm, far_cols_hbm, coupling_hbm,
    out,
    anomalies, order, far_rows, far_cols, bases, near, coupling, cols_all, halo, tree, one_hot, selector, chosen, table,
    turned, picked, near_field, placing, combined,
    small_sems, load_sems, near_sems, cols_send, cols_recv, halo_send, halo_recv, coef_send, coef_recv,
):
    me = lax.axis_index("row") * inner + lax.axis_index("col")
    width = leaves * leaf
    split = leaf // rank
    groups = members // split
    rows = NEED * groups
    per = leaf // rows
    blocks = n // per
    halves = tasks // LANES

    def at(index):
        return {"row": index // inner, "col": lax.rem(index, inner)}

    def peer(step):
        return lax.rem(me + step, n)

    barrier = pltpu.get_barrier_semaphore()

    def greet(step, carry):
        pl.semaphore_signal(barrier, inc=1, device_id=at(peer(step)), device_id_type=pl.DeviceIdType.MESH)
        return carry

    lax.fori_loop(1, n, greet, 0)

    small = []
    pairs = ((order_hbm, order), (anomalies_hbm, anomalies), (far_cols_hbm, far_cols), (far_rows_hbm, far_rows))
    for i, (source, target) in enumerate(pairs):
        small.append(pltpu.make_async_copy(source, target, small_sems.at[i]))
        small[-1].start()
    load_bases = pltpu.make_async_copy(bases_hbm, bases, load_sems.at[0])
    load_bases.start()
    quarter = leaves // 4
    loads = []
    for q in range(4):
        part = pl.ds(q * quarter, quarter)
        loads.append(pltpu.make_async_copy(near_hbm.at[part], near.at[part], near_sems.at[q]))
        loads[-1].start()
    load_coupling = pltpu.make_async_copy(coupling_hbm.at[0], coupling, load_sems.at[1])
    load_coupling.start()

    small[0].wait()
    position = order[...]
    low = position % leaf
    high = position // leaf
    for c in range(leaves):
        piece = slice(c * leaf, (c + 1) * leaf)
        one_hot[:, piece] = flag(iota((leaf, leaf), 0) == low[:, piece])

    pl.semaphore_wait(barrier, n - 1)

    def cols_copy(step):
        return pltpu.make_async_remote_copy(
            src_ref=far_cols_hbm, dst_ref=cols_all.at[me],
            send_sem=cols_send.at[step], recv_sem=cols_recv.at[step],
            device_id=at(peer(step)), device_id_type=pl.DeviceIdType.MESH,
        )

    def cols_start(step, carry):
        cols_copy(step).start()
        return carry

    lax.fori_loop(1, n, cols_start, 0)
    cols_all[me] = jnp.full((1, tasks), -1, jnp.int32)

    small[1].wait()
    stacked = jnp.concatenate(
        [anomalies[:, s * leaf : (s + 1) * leaf] for s in range(leaves)], axis=0
    )
    for c in range(leaves):
        piece = slice(c * leaf, (c + 1) * leaf)
        spread = dot(stacked, one_hot[:, piece])
        where_high = high[:, piece]
        total = jnp.zeros((members, leaf), F32)
        for s in range(leaves):
            total = total + jnp.where(where_high == s, spread[s * members : (s + 1) * members], 0.0)
        tree[:, piece] = total.astype(BF16)

    to_next = pltpu.make_async_remote_copy(
        src_ref=tree.at[:, pl.ds((leaves - 1) * leaf, leaf)], dst_ref=halo.at[0],
        send_sem=halo_send.at[0], recv_sem=halo_recv.at[0],
        device_id=at(peer(1)), device_id_type=pl.DeviceIdType.MESH,
    )
    to_before = pltpu.make_async_remote_copy(
        src_ref=tree.at[:, pl.ds(0, leaf)], dst_ref=halo.at[1],
        send_sem=halo_send.at[1], recv_sem=halo_recv.at[1],
        device_id=at(peer(n - 1)), device_id_type=pl.DeviceIdType.MESH,
    )
    to_next.start()
    to_before.start()

    load_bases.wait()
    upward = jnp.concatenate(
        [dot_last(tree[:, t * leaf : (t + 1) * leaf], bases[t]) for t in range(leaves)], axis=0
    ).astype(BF16)
    repeat = flag(iota((rank, leaf), 0) == iota((rank, leaf), 1) % rank)
    square = (leaf, leaf)
    row, col = iota(square, 0), iota(square, 1)
    spread = dot(upward, repeat)
    placed = jnp.where(row % split == col // rank, spread, 0.0).astype(BF16)

    same = row // rows == col // rows
    gather = flag(same)
    earlier = flag(same & (col < row))
    ones = jnp.ones((tasks, leaf), BF16)
    slot = (row % rows) // groups + 1
    group_row = row % groups

    def ranks(hits):
        needed = jnp.minimum(dot(hits, ones), 1.0)
        return needed, dot(earlier, needed.astype(BF16)) + 1.0

    def cols_wait(step, carry):
        cols_copy(step).wait()
        return carry

    lax.fori_loop(1, n, cols_wait, 0)
    slot_f = slot.astype(F32)
    diagonal = row % leaves == col // members
    same_group = group_row == (col % members) // split
    for c in range(blocks):
        wanted = jnp.concatenate(
            [jnp.broadcast_to(cols_all[c * per + d], (leaves, tasks)) for d in range(per)], axis=0
        )
        hits = flag(wanted == iota((leaf, tasks), 0) % leaves + me * leaves)
        needed, numbered = ranks(hits)
        values = jnp.where(diagonal, needed * numbered, 0.0).astype(BF16)
        rank_of = dot(gather, values)
        selection = flag((rank_of == slot_f) & same_group)
        chosen[c * leaf : (c + 1) * leaf, :] = dot(selection, placed).astype(BF16)

    def coef_copy(step):
        there = peer(step)
        return pltpu.make_async_remote_copy(
            src_ref=chosen.at[pl.ds(pl.multiple_of(there * rows, rows), rows)],
            dst_ref=table.at[pl.ds(pl.multiple_of(me * rows, rows), rows)],
            send_sem=coef_send.at[step], recv_sem=coef_recv.at[step],
            device_id=at(there), device_id_type=pl.DeviceIdType.MESH,
        )

    def coef_start(step, carry):
        coef_copy(step).start()
        return carry

    lax.fori_loop(1, n, coef_start, 0)
    table[pl.ds(pl.multiple_of(me * rows, rows), rows), :] = jnp.zeros((rows, leaf), BF16)

    small[2].wait()
    small[3].wait()
    own = far_cols[...]
    for c in range(blocks):
        hits = own == iota((leaf, tasks), 0) + c * leaf
        needed, numbered = ranks(flag(hits))
        rank_of = dot(gather, jnp.where(hits, numbered, 0.0).astype(BF16))
        selector[c * leaf : (c + 1) * leaf, :] = jnp.where(rank_of == slot_f, 1.0, 0.0).astype(BF16)
    placing[...] = flag(far_rows[...] == iota((leaf, tasks), 0) // members + me * leaves)

    to_next.wait()
    to_before.wait()
    before = jnp.where(me > 0, halo[0].astype(F32), 0.0).astype(BF16)
    after = jnp.where(me < n - 1, halo[1].astype(F32), 0.0).astype(BF16)
    for t in range(leaves):
        if t % quarter == 0:
            loads[t // quarter].wait()
        total = jnp.zeros((members, leaf), F32)
        for j in range(3):
            s = t + j - 1
            if s < 0:
                x = before
            elif s >= leaves:
                x = after
            else:
                x = tree[:, s * leaf : (s + 1) * leaf]
            total = total + dot_last(x, near[t, j])
        near_field[:, t * leaf : (t + 1) * leaf] = total

    load_coupling.wait()
    identity = flag(row == col)
    for c in range(rank * rank // leaf):
        piece = slice(c * leaf, (c + 1) * leaf)
        flipped = dot_last(identity, coupling[:, piece])
        for h in range(halves):
            turned[h, piece, :] = flipped[:, h * LANES : (h + 1) * LANES]

    def coef_wait(step, carry):
        coef_copy(step).wait()
        return carry

    lax.fori_loop(1, n, coef_wait, 0)
    for g in range(groups):
        total = jnp.zeros((leaf, tasks), F32)
        for c in range(blocks):
            chunk = slice(c * leaf, (c + 1) * leaf)
            taken = jnp.where(group_row == g, selector[chunk, :].astype(F32), 0.0).astype(BF16)
            total = total + lax.dot_general(table[chunk, :], taken, FIRST, preferred_element_type=F32)
        for h in range(halves):
            picked[h, g * leaf : (g + 1) * leaf, :] = total[:, h * LANES : (h + 1) * LANES]

    together = 4

    def advance(step, total):
        left = []
        right = []
        for u in range(together):
            b = step * together + u
            for h in range(halves):
                values = picked[h, pl.ds(b, members, stride=rank), :].astype(BF16)
                mask = placing[:, h * LANES : (h + 1) * LANES]
                left.append(jnp.concatenate([values] * leaves, axis=0) * mask)
                right.append(turned[h, pl.ds(b, rank, stride=rank), :].astype(BF16))
        return total + dot_last(jnp.concatenate(left, axis=1), jnp.concatenate(right, axis=1))

    far = lax.fori_loop(0, rank // together, advance, jnp.zeros((leaves * members, rank), F32))
    far = far.astype(BF16)
    for t in range(leaves):
        piece = slice(t * leaf, (t + 1) * leaf)
        value = near_field[:, piece] + dot(far[t * members : (t + 1) * members], bases[t])
        combined[:, piece] = value.astype(BF16)

    total = jnp.zeros((leaves * members, leaf), F32)
    for c in range(leaves):
        piece = slice(c * leaf, (c + 1) * leaf)
        values = combined[:, piece].astype(F32)
        where_high = high[:, piece]
        left = jnp.concatenate(
            [jnp.where(where_high == s, values, 0.0).astype(BF16) for s in range(leaves)], axis=0
        )
        total = total + dot_last(left, one_hot[:, piece])
    for s in range(leaves):
        out[:, s * leaf : (s + 1) * leaf] = total[s * members : (s + 1) * members].astype(BF16)


def body(n, inner, anomalies, order, bases, near_blocks, far_rows, far_cols, coupling):
    members, points = anomalies.shape
    leaves, rank, leaf = bases.shape
    tasks = far_cols.shape[1]
    rows = NEED * members * rank // leaf
    vmem = pl.BlockSpec(memory_space=pltpu.VMEM)
    hbm = pl.BlockSpec(memory_space=pltpu.HBM)
    dma = pltpu.SemaphoreType.DMA
    return pl.pallas_call(
        functools.partial(kernel, n, inner, members, leaves, rank, leaf, tasks),
        out_shape=jax.ShapeDtypeStruct((members, points), BF16),
        in_specs=[hbm] * 7,
        out_specs=vmem,
        scratch_shapes=[
            pltpu.VMEM(anomalies.shape, BF16),
            pltpu.VMEM(order.shape, jnp.int32),
            pltpu.VMEM(far_rows.shape, jnp.int32),
            pltpu.VMEM(far_cols.shape, jnp.int32),
            pltpu.VMEM(bases.shape, BF16),
            pltpu.VMEM(near_blocks.shape, BF16),
            pltpu.VMEM((tasks, rank * rank), BF16),
            pltpu.VMEM((n, 1, tasks), jnp.int32),
            pltpu.VMEM((2, members, leaf), BF16),
            pltpu.VMEM((members, points), BF16),
            pltpu.VMEM((leaf, points), BF16),
            pltpu.VMEM((n * rows, tasks), BF16),
            pltpu.VMEM((n * rows, leaf), BF16),
            pltpu.VMEM((n * rows, leaf), BF16),
            pltpu.VMEM((tasks // LANES, rank * rank, LANES), F32),
            pltpu.VMEM((tasks // LANES, members * rank, LANES), F32),
            pltpu.VMEM((members, points), F32),
            pltpu.VMEM((leaves * members, tasks), BF16),
            pltpu.VMEM((members, points), BF16),
            dma((4,)), dma((2,)), dma((4,)), dma((n,)), dma((n,)), dma((2,)), dma((2,)), dma((n,)), dma((n,)),
        ],
        compiler_params=pltpu.CompilerParams(
            collective_id=0, has_side_effects=True, vmem_limit_bytes=60 * 1024 * 1024
        ),
    )(anomalies, order, bases, near_blocks, far_rows, far_cols, coupling)


def solution(mesh):
    rows, inner = mesh.shape["row"], mesh.shape["col"]
    spread = ("row", "col")
    in_specs = (
        P("group", spread),
        P(spread, None),
        P(spread, None, None),
        P(spread, None, None, None),
        P(spread, None),
        P(spread, None),
        P(spread, None, None),
    )
    return jax.shard_map(
        functools.partial(body, rows * inner, inner),
        mesh=mesh, in_specs=in_specs, out_specs=P("group", spread), check_vma=False,
    )
```

```python
import functools

import jax
import jax.numpy as jnp
from jax import lax
from jax.experimental import pallas as pl
from jax.experimental.pallas import tpu as pltpu
from jax.sharding import PartitionSpec as P

NEED = 4
LANES = 128
F32 = jnp.float32
BF16 = jnp.bfloat16
LAST = (((1,), (1,)), ((), ()))
FIRST = (((0,), (0,)), ((), ()))


def dot(x, y):
    return jnp.dot(x, y, preferred_element_type=F32)


def dot_last(x, y):
    return lax.dot_general(x, y, LAST, preferred_element_type=F32)


def iota(shape, dim):
    return lax.broadcasted_iota(jnp.int32, shape, dim)


def flag(condition):
    return jnp.where(condition, 1.0, 0.0).astype(BF16)


def kernel(
    n, inner, members, leaves, rank, leaf, tasks,
    anomalies_hbm, order_hbm, bases_hbm, near_hbm, far_rows_hbm, far_cols_hbm, coupling_hbm,
    out,
    anomalies, order, far_rows, far_cols, bases, near, coupling, cols_all, halo, tree, one_hot, selector, chosen, table,
    turned, picked, near_field, placing, combined,
    small_sems, load_sems, near_sems, cols_send, cols_recv, halo_send, halo_recv, coef_send, coef_recv,
):
    me = lax.axis_index("row") * inner + lax.axis_index("col")
    width = leaves * leaf
    split = leaf // rank
    groups = members // split
    rows = NEED * groups
    per = leaf // rows
    blocks = n // per
    halves = tasks // LANES

    def at(index):
        return {"row": index // inner, "col": lax.rem(index, inner)}

    def peer(step):
        return lax.rem(me + step, n)

    barrier = pltpu.get_barrier_semaphore()

    def greet(step, carry):
        pl.semaphore_signal(barrier, inc=1, device_id=at(peer(step)), device_id_type=pl.DeviceIdType.MESH)
        return carry

    lax.fori_loop(1, n, greet, 0)

    small = []
    pairs = ((order_hbm, order), (anomalies_hbm, anomalies), (far_cols_hbm, far_cols), (far_rows_hbm, far_rows))
    for i, (source, target) in enumerate(pairs):
        small.append(pltpu.make_async_copy(source, target, small_sems.at[i]))
        small[-1].start()
    load_bases = pltpu.make_async_copy(bases_hbm, bases, load_sems.at[0])
    load_bases.start()
    quarter = leaves // 4
    loads = []
    for q in range(4):
        part = pl.ds(q * quarter, quarter)
        loads.append(pltpu.make_async_copy(near_hbm.at[part], near.at[part], near_sems.at[q]))
        loads[-1].start()
    load_coupling = pltpu.make_async_copy(coupling_hbm.at[0], coupling, load_sems.at[1])
    load_coupling.start()

    small[0].wait()
    position = order[...]
    low = position % leaf
    high = position // leaf
    for c in range(leaves):
        piece = slice(c * leaf, (c + 1) * leaf)
        one_hot[:, piece] = flag(iota((leaf, leaf), 0) == low[:, piece])

    pl.semaphore_wait(barrier, n - 1)

    def cols_copy(step):
        return pltpu.make_async_remote_copy(
            src_ref=far_cols_hbm, dst_ref=cols_all.at[me],
            send_sem=cols_send.at[step], recv_sem=cols_recv.at[step],
            device_id=at(peer(step)), device_id_type=pl.DeviceIdType.MESH,
        )

    def cols_start(step, carry):
        cols_copy(step).start()
        return carry

    lax.fori_loop(1, n, cols_start, 0)
    cols_all[me] = jnp.full((1, tasks), -1, jnp.int32)

    small[1].wait()
    stacked = jnp.concatenate(
        [anomalies[:, s * leaf : (s + 1) * leaf] for s in range(leaves)], axis=0
    )
    for c in range(leaves):
        piece = slice(c * leaf, (c + 1) * leaf)
        spread = dot(stacked, one_hot[:, piece])
        where_high = high[:, piece]
        total = jnp.zeros((members, leaf), F32)
        for s in range(leaves):
            total = total + jnp.where(where_high == s, spread[s * members : (s + 1) * members], 0.0)
        tree[:, piece] = total.astype(BF16)

    to_next = pltpu.make_async_remote_copy(
        src_ref=tree.at[:, pl.ds((leaves - 1) * leaf, leaf)], dst_ref=halo.at[0],
        send_sem=halo_send.at[0], recv_sem=halo_recv.at[0],
        device_id=at(peer(1)), device_id_type=pl.DeviceIdType.MESH,
    )
    to_before = pltpu.make_async_remote_copy(
        src_ref=tree.at[:, pl.ds(0, leaf)], dst_ref=halo.at[1],
        send_sem=halo_send.at[1], recv_sem=halo_recv.at[1],
        device_id=at(peer(n - 1)), device_id_type=pl.DeviceIdType.MESH,
    )
    to_next.start()
    to_before.start()

    load_bases.wait()
    upward = jnp.concatenate(
        [dot_last(tree[:, t * leaf : (t + 1) * leaf], bases[t]) for t in range(leaves)], axis=0
    ).astype(BF16)
    repeat = flag(iota((rank, leaf), 0) == iota((rank, leaf), 1) % rank)
    square = (leaf, leaf)
    row, col = iota(square, 0), iota(square, 1)
    spread = dot(upward, repeat)
    placed = jnp.where(row % split == col // rank, spread, 0.0).astype(BF16)

    same = row // rows == col // rows
    gather = flag(same)
    earlier = flag(same & (col < row))
    ones = jnp.ones((tasks, leaf), BF16)
    slot = (row % rows) // groups + 1
    group_row = row % groups

    def ranks(hits):
        needed = jnp.minimum(dot(hits, ones), 1.0)
        return needed, dot(earlier, needed.astype(BF16)) + 1.0

    def cols_wait(step, carry):
        cols_copy(step).wait()
        return carry

    lax.fori_loop(1, n, cols_wait, 0)
    slot_f = slot.astype(F32)
    diagonal = row % leaves == col // members
    same_group = group_row == (col % members) // split
    for c in range(blocks):
        wanted = jnp.concatenate(
            [jnp.broadcast_to(cols_all[c * per + d], (leaves, tasks)) for d in range(per)], axis=0
        )
        hits = flag(wanted == iota((leaf, tasks), 0) % leaves + me * leaves)
        needed, numbered = ranks(hits)
        values = jnp.where(diagonal, needed * numbered, 0.0).astype(BF16)
        rank_of = dot(gather, values)
        selection = flag((rank_of == slot_f) & same_group)
        chosen[c * leaf : (c + 1) * leaf, :] = dot(selection, placed).astype(BF16)

    def coef_copy(step):
        there = peer(step)
        return pltpu.make_async_remote_copy(
            src_ref=chosen.at[pl.ds(pl.multiple_of(there * rows, rows), rows)],
            dst_ref=table.at[pl.ds(pl.multiple_of(me * rows, rows), rows)],
            send_sem=coef_send.at[step], recv_sem=coef_recv.at[step],
            device_id=at(there), device_id_type=pl.DeviceIdType.MESH,
        )

    def coef_start(step, carry):
        coef_copy(step).start()
        return carry

    lax.fori_loop(1, n, coef_start, 0)
    table[pl.ds(pl.multiple_of(me * rows, rows), rows), :] = jnp.zeros((rows, leaf), BF16)

    small[2].wait()
    small[3].wait()
    own = far_cols[...]
    for c in range(blocks):
        hits = own == iota((leaf, tasks), 0) + c * leaf
        needed, numbered = ranks(flag(hits))
        rank_of = dot(gather, jnp.where(hits, numbered, 0.0).astype(BF16))
        selector[c * leaf : (c + 1) * leaf, :] = jnp.where(rank_of == slot_f, 1.0, 0.0).astype(BF16)
    placing[...] = flag(far_rows[...] == iota((leaf, tasks), 0) // members + me * leaves)

    to_next.wait()
    to_before.wait()
    before = jnp.where(me > 0, halo[0].astype(F32), 0.0).astype(BF16)
    after = jnp.where(me < n - 1, halo[1].astype(F32), 0.0).astype(BF16)
    for t in range(leaves):
        if t % quarter == 0:
            loads[t // quarter].wait()
        total = jnp.zeros((members, leaf), F32)
        for j in range(3):
            s = t + j - 1
            if s < 0:
                x = before
            elif s >= leaves:
                x = after
            else:
                x = tree[:, s * leaf : (s + 1) * leaf]
            total = total + dot_last(x, near[t, j])
        near_field[:, t * leaf : (t + 1) * leaf] = total

    load_coupling.wait()
    identity = flag(row == col)
    for c in range(rank * rank // leaf):
        piece = slice(c * leaf, (c + 1) * leaf)
        flipped = dot_last(identity, coupling[:, piece])
        for h in range(halves):
            turned[h, piece, :] = flipped[:, h * LANES : (h + 1) * LANES]

    def coef_wait(step, carry):
        coef_copy(step).wait()
        return carry

    lax.fori_loop(1, n, coef_wait, 0)
    for g in range(groups):
        total = jnp.zeros((leaf, tasks), F32)
        for c in range(blocks):
            chunk = slice(c * leaf, (c + 1) * leaf)
            taken = jnp.where(group_row == g, selector[chunk, :].astype(F32), 0.0).astype(BF16)
            total = total + lax.dot_general(table[chunk, :], taken, FIRST, preferred_element_type=F32)
        for h in range(halves):
            picked[h, g * leaf : (g + 1) * leaf, :] = total[:, h * LANES : (h + 1) * LANES]

    together = 32

    def advance(step, total):
        left = []
        right = []
        for u in range(together):
            b = step * together + u
            for h in range(halves):
                values = picked[h, pl.ds(b, members, stride=rank), :].astype(BF16)
                mask = placing[:, h * LANES : (h + 1) * LANES]
                left.append(jnp.concatenate([values] * leaves, axis=0) * mask)
                right.append(turned[h, pl.ds(b, rank, stride=rank), :].astype(BF16))
        return total + dot_last(jnp.concatenate(right, axis=1), jnp.concatenate(left, axis=1))

    far = lax.fori_loop(0, rank // together, advance, jnp.zeros((rank, leaves * members), F32))
    far = far.T.astype(BF16)
    for t in range(leaves):
        piece = slice(t * leaf, (t + 1) * leaf)
        value = near_field[:, piece] + dot(far[t * members : (t + 1) * members], bases[t])
        combined[:, piece] = value.astype(BF16)

    total = jnp.zeros((leaves * members, leaf), F32)
    for c in range(leaves):
        piece = slice(c * leaf, (c + 1) * leaf)
        values = combined[:, piece].astype(F32)
        where_high = high[:, piece]
        left = jnp.concatenate(
            [jnp.where(where_high == s, values, 0.0).astype(BF16) for s in range(leaves)], axis=0
        )
        total = total + dot_last(left, one_hot[:, piece])
    for s in range(leaves):
        out[:, s * leaf : (s + 1) * leaf] = total[s * members : (s + 1) * members].astype(BF16)


def body(n, inner, anomalies, order, bases, near_blocks, far_rows, far_cols, coupling):
    members, points = anomalies.shape
    leaves, rank, leaf = bases.shape
    tasks = far_cols.shape[1]
    rows = NEED * members * rank // leaf
    vmem = pl.BlockSpec(memory_space=pltpu.VMEM)
    hbm = pl.BlockSpec(memory_space=pltpu.HBM)
    dma = pltpu.SemaphoreType.DMA
    return pl.pallas_call(
        functools.partial(kernel, n, inner, members, leaves, rank, leaf, tasks),
        out_shape=jax.ShapeDtypeStruct((members, points), BF16),
        in_specs=[hbm] * 7,
        out_specs=vmem,
        scratch_shapes=[
            pltpu.VMEM(anomalies.shape, BF16),
            pltpu.VMEM(order.shape, jnp.int32),
            pltpu.VMEM(far_rows.shape, jnp.int32),
            pltpu.VMEM(far_cols.shape, jnp.int32),
            pltpu.VMEM(bases.shape, BF16),
            pltpu.VMEM(near_blocks.shape, BF16),
            pltpu.VMEM((tasks, rank * rank), BF16),
            pltpu.VMEM((n, 1, tasks), jnp.int32),
            pltpu.VMEM((2, members, leaf), BF16),
            pltpu.VMEM((members, points), BF16),
            pltpu.VMEM((leaf, points), BF16),
            pltpu.VMEM((n * rows, tasks), BF16),
            pltpu.VMEM((n * rows, leaf), BF16),
            pltpu.VMEM((n * rows, leaf), BF16),
            pltpu.VMEM((tasks // LANES, rank * rank, LANES), F32),
            pltpu.VMEM((tasks // LANES, members * rank, LANES), F32),
            pltpu.VMEM((members, points), F32),
            pltpu.VMEM((leaves * members, tasks), BF16),
            pltpu.VMEM((members, points), BF16),
            dma((4,)), dma((2,)), dma((4,)), dma((n,)), dma((n,)), dma((2,)), dma((2,)), dma((n,)), dma((n,)),
        ],
        compiler_params=pltpu.CompilerParams(
            collective_id=0, has_side_effects=True, vmem_limit_bytes=60 * 1024 * 1024
        ),
    )(anomalies, order, bases, near_blocks, far_rows, far_cols, coupling)


def solution(mesh):
    rows, inner = mesh.shape["row"], mesh.shape["col"]
    spread = ("row", "col")
    in_specs = (
        P("group", spread),
        P(spread, None),
        P(spread, None, None),
        P(spread, None, None, None),
        P(spread, None),
        P(spread, None),
        P(spread, None, None),
    )
    return jax.shard_map(
        functools.partial(body, rows * inner, inner),
        mesh=mesh, in_specs=in_specs, out_specs=P("group", spread), check_vma=False,
    )
```

```python
import functools

import jax
import jax.numpy as jnp
from jax import lax
from jax.experimental import pallas as pl
from jax.experimental.pallas import tpu as pltpu
from jax.sharding import PartitionSpec as P

NEED = 4
LANES = 128
F32 = jnp.float32
BF16 = jnp.bfloat16
LAST = (((1,), (1,)), ((), ()))
FIRST = (((0,), (0,)), ((), ()))


def dot(x, y):
    return jnp.dot(x, y, preferred_element_type=F32)


def dot_last(x, y):
    return lax.dot_general(x, y, LAST, preferred_element_type=F32)


def iota(shape, dim):
    return lax.broadcasted_iota(jnp.int32, shape, dim)


def flag(condition):
    return jnp.where(condition, 1.0, 0.0).astype(BF16)


def kernel(
    n, inner, members, leaves, rank, leaf, tasks,
    anomalies_hbm, order_hbm, bases_hbm, near_hbm, far_rows_hbm, far_cols_hbm, coupling_hbm,
    out,
    anomalies, order, far_rows, far_cols, bases, near, coupling, cols_all, halo, tree, one_hot, selector, chosen, table,
    placed, turned, picked, near_field, placing, combined,
    small_sems, load_sems, near_sems, cols_send, cols_recv, halo_send, halo_recv, coef_send, coef_recv,
):
    me = lax.axis_index("row") * inner + lax.axis_index("col")
    width = leaves * leaf
    split = leaf // rank
    groups = members // split
    rows = NEED * groups
    per = leaf // rows
    blocks = n // per
    halves = tasks // LANES

    def at(index):
        return {"row": index // inner, "col": lax.rem(index, inner)}

    def peer(step):
        return lax.rem(me + step, n)

    barrier = pltpu.get_barrier_semaphore()

    def greet(step, carry):
        pl.semaphore_signal(barrier, inc=1, device_id=at(peer(step)), device_id_type=pl.DeviceIdType.MESH)
        return carry

    lax.fori_loop(1, n, greet, 0)

    small = []
    pairs = ((order_hbm, order), (anomalies_hbm, anomalies), (far_cols_hbm, far_cols), (far_rows_hbm, far_rows))
    for i, (source, target) in enumerate(pairs):
        small.append(pltpu.make_async_copy(source, target, small_sems.at[i]))
        small[-1].start()
    load_bases = pltpu.make_async_copy(bases_hbm, bases, load_sems.at[0])
    load_bases.start()
    quarter = leaves // 4
    loads = []
    for q in range(4):
        part = pl.ds(q * quarter, quarter)
        loads.append(pltpu.make_async_copy(near_hbm.at[part], near.at[part], near_sems.at[q]))
        loads[-1].start()
    load_coupling = pltpu.make_async_copy(coupling_hbm.at[0], coupling, load_sems.at[1])
    load_coupling.start()

    square = (leaf, leaf)
    row, col = iota(square, 0), iota(square, 1)
    early = me < n // 2

    def upward_pass():
        small[0].wait()
        position = order[...]
        low = position % leaf
        high = position // leaf
        for c in range(leaves):
            piece = slice(c * leaf, (c + 1) * leaf)
            one_hot[:, piece] = flag(iota((leaf, leaf), 0) == low[:, piece])

        small[1].wait()
        stacked = jnp.concatenate(
            [anomalies[:, s * leaf : (s + 1) * leaf] for s in range(leaves)], axis=0
        )
        for c in range(leaves):
            piece = slice(c * leaf, (c + 1) * leaf)
            spread = dot(stacked, one_hot[:, piece])
            where_high = high[:, piece]
            total = jnp.zeros((members, leaf), F32)
            for s in range(leaves):
                total = total + jnp.where(where_high == s, spread[s * members : (s + 1) * members], 0.0)
            tree[:, piece] = total.astype(BF16)

        load_bases.wait()
        upward = jnp.concatenate(
            [dot_last(tree[:, t * leaf : (t + 1) * leaf], bases[t]) for t in range(leaves)], axis=0
        ).astype(BF16)
        repeat = flag(iota((rank, leaf), 0) == iota((rank, leaf), 1) % rank)
        spread = dot(upward, repeat)
        placed[...] = jnp.where(row % split == col // rank, spread, 0.0).astype(BF16)

    @pl.when(early)
    def _():
        upward_pass()

    pl.semaphore_wait(barrier, n - 1)

    def cols_copy(step):
        return pltpu.make_async_remote_copy(
            src_ref=far_cols_hbm, dst_ref=cols_all.at[me],
            send_sem=cols_send.at[step], recv_sem=cols_recv.at[step],
            device_id=at(peer(step)), device_id_type=pl.DeviceIdType.MESH,
        )

    def cols_start(step, carry):
        cols_copy(step).start()
        return carry

    lax.fori_loop(1, n, cols_start, 0)
    cols_all[me] = jnp.full((1, tasks), -1, jnp.int32)

    @pl.when(jnp.logical_not(early))
    def _():
        upward_pass()

    to_next = pltpu.make_async_remote_copy(
        src_ref=tree.at[:, pl.ds((leaves - 1) * leaf, leaf)], dst_ref=halo.at[0],
        send_sem=halo_send.at[0], recv_sem=halo_recv.at[0],
        device_id=at(peer(1)), device_id_type=pl.DeviceIdType.MESH,
    )
    to_before = pltpu.make_async_remote_copy(
        src_ref=tree.at[:, pl.ds(0, leaf)], dst_ref=halo.at[1],
        send_sem=halo_send.at[1], recv_sem=halo_recv.at[1],
        device_id=at(peer(n - 1)), device_id_type=pl.DeviceIdType.MESH,
    )
    to_next.start()
    to_before.start()

    same = row // rows == col // rows
    gather = flag(same)
    earlier = flag(same & (col < row))
    ones = jnp.ones((tasks, leaf), BF16)
    slot = (row % rows) // groups + 1
    group_row = row % groups

    def ranks(hits):
        needed = jnp.minimum(dot(hits, ones), 1.0)
        return needed, dot(earlier, needed.astype(BF16)) + 1.0

    def cols_wait(step, carry):
        cols_copy(step).wait()
        return carry

    lax.fori_loop(1, n, cols_wait, 0)
    slot_f = slot.astype(F32)
    diagonal = row % leaves == col // members
    same_group = group_row == (col % members) // split
    for c in range(blocks):
        wanted = jnp.concatenate(
            [jnp.broadcast_to(cols_all[c * per + d], (leaves, tasks)) for d in range(per)], axis=0
        )
        hits = flag(wanted == iota((leaf, tasks), 0) % leaves + me * leaves)
        needed, numbered = ranks(hits)
        values = jnp.where(diagonal, needed * numbered, 0.0).astype(BF16)
        rank_of = dot(gather, values)
        selection = flag((rank_of == slot_f) & same_group)
        chosen[c * leaf : (c + 1) * leaf, :] = dot(selection, placed[...]).astype(BF16)

    def coef_copy(step):
        there = peer(step)
        return pltpu.make_async_remote_copy(
            src_ref=chosen.at[pl.ds(pl.multiple_of(there * rows, rows), rows)],
            dst_ref=table.at[pl.ds(pl.multiple_of(me * rows, rows), rows)],
            send_sem=coef_send.at[step], recv_sem=coef_recv.at[step],
            device_id=at(there), device_id_type=pl.DeviceIdType.MESH,
        )

    def coef_start(step, carry):
        coef_copy(step).start()
        return carry

    lax.fori_loop(1, n, coef_start, 0)
    table[pl.ds(pl.multiple_of(me * rows, rows), rows), :] = jnp.zeros((rows, leaf), BF16)

    small[2].wait()
    small[3].wait()
    own = far_cols[...]
    for c in range(blocks):
        hits = own == iota((leaf, tasks), 0) + c * leaf
        needed, numbered = ranks(flag(hits))
        rank_of = dot(gather, jnp.where(hits, numbered, 0.0).astype(BF16))
        selector[c * leaf : (c + 1) * leaf, :] = jnp.where(rank_of == slot_f, 1.0, 0.0).astype(BF16)
    placing[...] = flag(far_rows[...] == iota((leaf, tasks), 0) // members + me * leaves)

    to_next.wait()
    to_before.wait()
    before = jnp.where(me > 0, halo[0].astype(F32), 0.0).astype(BF16)
    after = jnp.where(me < n - 1, halo[1].astype(F32), 0.0).astype(BF16)
    for t in range(leaves):
        if t % quarter == 0:
            loads[t // quarter].wait()
        total = jnp.zeros((members, leaf), F32)
        for j in range(3):
            s = t + j - 1
            if s < 0:
                x = before
            elif s >= leaves:
                x = after
            else:
                x = tree[:, s * leaf : (s + 1) * leaf]
            total = total + dot_last(x, near[t, j])
        near_field[:, t * leaf : (t + 1) * leaf] = total

    load_coupling.wait()
    identity = flag(row == col)
    for c in range(rank * rank // leaf):
        piece = slice(c * leaf, (c + 1) * leaf)
        flipped = dot_last(identity, coupling[:, piece])
        for h in range(halves):
            turned[h, piece, :] = flipped[:, h * LANES : (h + 1) * LANES]

    def coef_wait(step, carry):
        coef_copy(step).wait()
        return carry

    lax.fori_loop(1, n, coef_wait, 0)
    for g in range(groups):
        total = jnp.zeros((leaf, tasks), F32)
        for c in range(blocks):
            chunk = slice(c * leaf, (c + 1) * leaf)
            taken = jnp.where(group_row == g, selector[chunk, :].astype(F32), 0.0).astype(BF16)
            total = total + lax.dot_general(table[chunk, :], taken, FIRST, preferred_element_type=F32)
        for h in range(halves):
            picked[h, g * leaf : (g + 1) * leaf, :] = total[:, h * LANES : (h + 1) * LANES]

    together = 32

    def advance(step, total):
        left = []
        right = []
        for u in range(together):
            b = step * together + u
            for h in range(halves):
                values = picked[h, pl.ds(b, members, stride=rank), :].astype(BF16)
                mask = placing[:, h * LANES : (h + 1) * LANES]
                left.append(jnp.concatenate([values] * leaves, axis=0) * mask)
                right.append(turned[h, pl.ds(b, rank, stride=rank), :].astype(BF16))
        return total + dot_last(jnp.concatenate(right, axis=1), jnp.concatenate(left, axis=1))

    far = lax.fori_loop(0, rank // together, advance, jnp.zeros((rank, leaves * members), F32))
    far = far.T.astype(BF16)
    for t in range(leaves):
        piece = slice(t * leaf, (t + 1) * leaf)
        value = near_field[:, piece] + dot(far[t * members : (t + 1) * members], bases[t])
        combined[:, piece] = value.astype(BF16)

    total = jnp.zeros((leaves * members, leaf), F32)
    for c in range(leaves):
        piece = slice(c * leaf, (c + 1) * leaf)
        values = combined[:, piece].astype(F32)
        where_high = order[:, piece] // leaf
        left = jnp.concatenate(
            [jnp.where(where_high == s, values, 0.0).astype(BF16) for s in range(leaves)], axis=0
        )
        total = total + dot_last(left, one_hot[:, piece])
    for s in range(leaves):
        out[:, s * leaf : (s + 1) * leaf] = total[s * members : (s + 1) * members].astype(BF16)


def body(n, inner, anomalies, order, bases, near_blocks, far_rows, far_cols, coupling):
    members, points = anomalies.shape
    leaves, rank, leaf = bases.shape
    tasks = far_cols.shape[1]
    rows = NEED * members * rank // leaf
    vmem = pl.BlockSpec(memory_space=pltpu.VMEM)
    hbm = pl.BlockSpec(memory_space=pltpu.HBM)
    dma = pltpu.SemaphoreType.DMA
    return pl.pallas_call(
        functools.partial(kernel, n, inner, members, leaves, rank, leaf, tasks),
        out_shape=jax.ShapeDtypeStruct((members, points), BF16),
        in_specs=[hbm] * 7,
        out_specs=vmem,
        scratch_shapes=[
            pltpu.VMEM(anomalies.shape, BF16),
            pltpu.VMEM(order.shape, jnp.int32),
            pltpu.VMEM(far_rows.shape, jnp.int32),
            pltpu.VMEM(far_cols.shape, jnp.int32),
            pltpu.VMEM(bases.shape, BF16),
            pltpu.VMEM(near_blocks.shape, BF16),
            pltpu.VMEM((tasks, rank * rank), BF16),
            pltpu.VMEM((n, 1, tasks), jnp.int32),
            pltpu.VMEM((2, members, leaf), BF16),
            pltpu.VMEM((members, points), BF16),
            pltpu.VMEM((leaf, points), BF16),
            pltpu.VMEM((n * rows, tasks), BF16),
            pltpu.VMEM((n * rows, leaf), BF16),
            pltpu.VMEM((n * rows, leaf), BF16),
            pltpu.VMEM((leaf, leaf), BF16),
            pltpu.VMEM((tasks // LANES, rank * rank, LANES), F32),
            pltpu.VMEM((tasks // LANES, members * rank, LANES), F32),
            pltpu.VMEM((members, points), F32),
            pltpu.VMEM((leaves * members, tasks), BF16),
            pltpu.VMEM((members, points), BF16),
            dma((4,)), dma((2,)), dma((4,)), dma((n,)), dma((n,)), dma((2,)), dma((2,)), dma((n,)), dma((n,)),
        ],
        compiler_params=pltpu.CompilerParams(
            collective_id=0, has_side_effects=True, vmem_limit_bytes=60 * 1024 * 1024
        ),
    )(anomalies, order, bases, near_blocks, far_rows, far_cols, coupling)


def solution(mesh):
    rows, inner = mesh.shape["row"], mesh.shape["col"]
    spread = ("row", "col")
    in_specs = (
        P("group", spread),
        P(spread, None),
        P(spread, None, None),
        P(spread, None, None, None),
        P(spread, None),
        P(spread, None),
        P(spread, None, None),
    )
    return jax.shard_map(
        functools.partial(body, rows * inner, inner),
        mesh=mesh, in_specs=in_specs, out_specs=P("group", spread), check_vma=False,
    )
```
